256 devices in a mesh: ctx: 32 (over z, x), head: 8 (over y, core).
Axes of the slice: x: 4, y: 4, z: 8, core: 2. Of those that a mesh axis runs over, the one named last changes fastest.
Arguments:
- queries: bfloat16 [16384, 8192], P(('ctx', 'head')), may hold values from -14 to 14
- key_vectors: bfloat16 [16384, 8192], P(('ctx', 'head')), may hold values from -14 to 14
- value_vectors: bfloat16 [16384, 8192], P(('ctx', 'head')), may hold values from -6 to 6
- out_grad: bfloat16 [16384, 8192], P(('ctx', 'head')), may hold values from -6 to 6
- chosen: int32 [32, 3], P('ctx'), may hold values from 0 to 30, as said below
Outputs:
- query_grad: bfloat16 [16384, 8192], P(('ctx', 'head'))
- key_grad: bfloat16 [16384, 8192], P(('ctx', 'head'))
- value_grad: bfloat16 [16384, 8192], P(('ctx', 'head'))
The draws below stay inside these ranges and needn't reach their ends.
Inputs may be any that keep to these rules, and one draw needn't show every extreme that they name: `chosen`: row b lists min(b, 3) different blocks below b; its first entry is block b - 1 when b >= 1; its other entries equal b and mark unused slots.
All inputs are finite; a program needn't handle non-finite values.
Results may differ from the reference program's by a relative error of at most 0.0099.
Values may be sent and summed in bfloat16 or wider, within the bound.
A program may use at most 128 MiB of HBM per device.

```python
import jax
import jax.numpy as jnp
from jax import lax

H = 64
HD = 128
BLOCK = 512
TOPK = 3
NBLK = 32
TOKENS = 16384


def draw_queries(key, part):
    key = jax.random.fold_in(key, 3)
    entries = jnp.clip(jax.random.normal(key, (TOKENS, H * HD), jnp.float32), -6.0, 6.0)
    return entries.astype(jnp.bfloat16)


def draw_key_vectors(key, part):
    key = jax.random.fold_in(key, 5)
    entries = jnp.clip(jax.random.normal(key, (TOKENS, H * HD), jnp.float32), -6.0, 6.0)
    return entries.astype(jnp.bfloat16)


def draw_chosen(key, part):
    key = jax.random.fold_in(key, 11)
    positions = jnp.arange(NBLK, dtype=jnp.int32)[:, None]
    columns = jnp.arange(NBLK, dtype=jnp.int32)[None, :]
    random_part = jax.random.randint(key, (NBLK, NBLK), 0, 65536, dtype=jnp.int32)
    scores = random_part * NBLK + columns
    scores = jnp.where(columns == positions - 1, 65536 * NBLK + NBLK, scores)
    scores = jnp.where(columns < positions, scores, -1 - columns)
    ignored, picked = lax.top_k(scores, TOPK)
    picked = picked.astype(jnp.int32)
    return jnp.where(picked < positions, picked, positions).astype(jnp.int32)


def levels(rng, dims, shards, low, high):
    factor_of, own = 1.0, jax.random.fold_in(rng, 6)
    for dim, shards_of in shards:
        draws = jnp.exp(jax.random.uniform(jax.random.fold_in(own, dim), (shards_of,), jnp.float32, low / len(shards), high / len(shards)))
        factor_of = factor_of * jnp.repeat(draws, dims[dim] // shards_of).reshape([-1 if axis == dim else 1 for axis in range(len(dims))])
    return factor_of


def bell_draw(own_key, dims, deviation, limit, cuts=(), held_as=jnp.bfloat16):
    values = jax.random.normal(own_key, dims, jnp.float32) * deviation
    if len(cuts) > 0:
        values = levels(own_key, dims, cuts, -0.22, 0.18) * values
    return jnp.clip(values, min=-limit, max=limit).astype(held_as)


def setup_inputs(seed: int = 0) -> dict:
    streams_of = jax.random.split(jax.random.key(seed), 6)
    queries = draw_queries(jax.random.fold_in(streams_of[5], 71), 0)
    key_vectors = draw_key_vectors(jax.random.fold_in(streams_of[5], 71), 0)
    value_vectors = bell_draw(streams_of[2], (TOKENS, H * HD), 1.0, 6.0, ((0, 256),))
    out_grad = bell_draw(streams_of[3], (TOKENS, H * HD), 1.0, 6.0, ((0, 256),))
    chosen = draw_chosen(jax.random.fold_in(streams_of[5], 71), 0)
    return {"queries": queries, "key_vectors": key_vectors, "value_vectors": value_vectors, "out_grad": out_grad, "chosen": chosen}


masked_score = -1.0e30


def attend(query_rows, key_rows, value_rows, grad_rows, visible, scaling):
    scores = jnp.dot(query_rows, key_rows.T, preferred_element_type=jnp.float32) * scaling
    scores = jnp.where(visible, scores, masked_score)
    largest = jnp.max(scores, axis=1, keepdims=True)
    totals = jnp.sum(jnp.exp(scores - largest), axis=1, keepdims=True)
    log_total = largest + jnp.log(totals)
    prob_rows = jnp.exp(scores - log_total)
    weights = prob_rows.astype(jnp.bfloat16)
    attended = jnp.dot(weights, value_rows, preferred_element_type=jnp.float32)
    row_delta = jnp.sum(grad_rows.astype(jnp.float32) * attended, axis=1, keepdims=True)
    dprobs = jnp.dot(grad_rows, value_rows.T, preferred_element_type=jnp.float32)
    dscores = (prob_rows * (dprobs - row_delta)).astype(jnp.bfloat16)
    query_part = (jnp.dot(dscores, key_rows, preferred_element_type=jnp.float32) * scaling).astype(jnp.bfloat16)
    key_part = jnp.dot(dscores.T, query_rows, preferred_element_type=jnp.float32) * scaling
    value_part = jnp.dot(weights.T, grad_rows, preferred_element_type=jnp.float32)
    return query_part, key_part, value_part


def reference(queries, key_vectors, value_vectors, out_grad, chosen):
    scaling = HD ** -0.5
    shaped = (NBLK, BLOCK, H, HD)
    query_blocks = queries.reshape(shaped)
    key_blocks = key_vectors.reshape(shaped)
    value_blocks = value_vectors.reshape(shaped)
    grad_blocks = out_grad.reshape(shaped)
    positions = jnp.arange(BLOCK, dtype=jnp.int32)
    causal = positions[:, None] >= positions[None, :]

    def per_block(running, block_index):
        key_sums, value_sums = running
        picked = chosen[block_index]
        slot_used = picked != block_index
        far_visible = jnp.broadcast_to(jnp.repeat(slot_used, BLOCK)[None, :], (BLOCK, TOPK * BLOCK))
        visible = jnp.concatenate([causal, far_visible], axis=1)
        key_rows = jnp.concatenate([key_blocks[block_index][None], key_blocks[picked]], axis=0)
        value_rows = jnp.concatenate([value_blocks[block_index][None], value_blocks[picked]], axis=0)
        key_heads = jnp.transpose(key_rows, (2, 0, 1, 3)).reshape(H, (1 + TOPK) * BLOCK, HD)
        value_heads = jnp.transpose(value_rows, (2, 0, 1, 3)).reshape(H, (1 + TOPK) * BLOCK, HD)
        query_heads = jnp.swapaxes(query_blocks[block_index], 0, 1)
        grad_heads = jnp.swapaxes(grad_blocks[block_index], 0, 1)

        def per_head(operands):
            return attend(operands[0], operands[1], operands[2], operands[3], visible, scaling)

        query_part, key_part, value_part = lax.map(per_head, (query_heads, key_heads, value_heads, grad_heads))
        key_sums = key_sums.at[block_index].add(jnp.swapaxes(key_part[:, :BLOCK], 0, 1))
        value_sums = value_sums.at[block_index].add(jnp.swapaxes(value_part[:, :BLOCK], 0, 1))
        key_far = jnp.transpose(key_part[:, BLOCK:].reshape(H, TOPK, BLOCK, HD), (1, 2, 0, 3))
        value_far = jnp.transpose(value_part[:, BLOCK:].reshape(H, TOPK, BLOCK, HD), (1, 2, 0, 3))
        key_far = lax.optimization_barrier(key_far.astype(jnp.bfloat16)).astype(jnp.float32)
        value_far = lax.optimization_barrier(value_far.astype(jnp.bfloat16)).astype(jnp.float32)
        for slot_index in range(TOPK):
            target = picked[slot_index]
            key_sums = key_sums.at[target].add(jnp.where(slot_used[slot_index], key_far[slot_index], 0.0))
            value_sums = value_sums.at[target].add(jnp.where(slot_used[slot_index], value_far[slot_index], 0.0))
        return (key_sums, value_sums), jnp.swapaxes(query_part, 0, 1)

    empty_sums = jnp.zeros(shaped, jnp.float32)
    final_sums, query_grad = lax.scan(per_block, (empty_sums, empty_sums), jnp.arange(NBLK, dtype=jnp.int32))
    flat_shape = (TOKENS, H * HD)
    key_grad = final_sums[0].astype(jnp.bfloat16).reshape(flat_shape)
    value_grad = final_sums[1].astype(jnp.bfloat16).reshape(flat_shape)
    return query_grad.reshape(flat_shape), key_grad, value_grad
```

```python
import functools

import jax
import jax.numpy as jnp
from jax import lax
from jax.experimental import pallas as pl
from jax.experimental.pallas import tpu as pltpu
from jax.sharding import PartitionSpec as P

H = 64
HD = 128
BLOCK = 512
TOPK = 3
CHUNKS = 4
PIECE = 16
MESH = pl.DeviceIdType.MESH
LOG2E = 1.4426950408889634
masked_score = -1e30


def mm(a, b, dims):
    return lax.dot_general(a, b, (dims, ((), ())), preferred_element_type=jnp.float32)


def kernel(
    nctx,
    nhead,
    q_in,
    k_in,
    v_in,
    g_in,
    chosen_ref,
    q_out,
    k_out,
    v_out,
    kv,
    qg,
    table,
    staging,
    far_grad,
    own_grad,
    parts,
    sums,
    back,
    prev_back,
    done,
    pick,
    unpick,
    score_scr,
    dprob_scr,
    my_list,
    lists,
    list_send,
    list_recv,
    in_send,
    in_recv,
    piece_send,
    piece_recv,
    prev_send,
    prev_recv,
    far_send,
    far_recv,
    grad_send,
    grad_recv,
    pgrad_send,
    pgrad_recv,
    sum_send,
    sum_recv,
    out_send,
    out_recv,
):
    c_me = lax.axis_index("ctx")
    h_me = lax.axis_index("head")
    lanes = kv.shape[-1]
    heads = lanes // HD
    rows = BLOCK // nhead
    group = lanes * CHUNKS
    scaling = HD ** (-0.5)
    factor = scaling * LOG2E
    next_ctx = lax.rem(c_me + 1, nctx)
    last_ctx = lax.rem(c_me + nctx - 1, nctx)

    def ctx_peers(body):
        def step(k, carry):
            body(lax.rem(c_me + k, nctx))
            return carry

        lax.fori_loop(1, nctx, step, 0)

    def head_peers(body):
        def step(k, carry):
            body(lax.rem(h_me + k, nhead))
            return carry

        lax.fori_loop(1, nhead, step, 0)

    def remote(src, dst, send, recv, c_to, h_to):
        return pltpu.make_async_remote_copy(
            src_ref=src,
            dst_ref=dst,
            send_sem=send,
            recv_sem=recv,
            device_id=(c_to, h_to),
            device_id_type=MESH,
        )

    def await_bytes(ref, sem):
        pltpu.make_async_copy(ref, ref, sem).wait()

    barrier = pltpu.get_barrier_semaphore()
    ctx_peers(lambda p: pl.semaphore_signal(barrier, inc=1, device_id=(p, h_me), device_id_type=MESH))
    head_peers(lambda p: pl.semaphore_signal(barrier, inc=1, device_id=(c_me, p), device_id_type=MESH))
    pl.semaphore_wait(barrier, nctx + nhead - 2)

    def slab_columns(peer, c):
        return pl.ds(pl.multiple_of(peer * group + c * lanes, 128), lanes)

    my_rows = pl.ds(pl.multiple_of(h_me * rows, rows), rows)

    def piece_rows(peer):
        return pl.ds(pl.multiple_of(peer * PIECE, PIECE), PIECE)

    def send_in(c, which, src, dst):
        head_peers(
            lambda p: remote(
                src.at[:, slab_columns(p, c)],
                dst.at[my_rows],
                in_send.at[c, which],
                in_recv.at[c, which],
                c_me,
                p,
            ).start()
        )
        pltpu.make_async_copy(
            src.at[:, slab_columns(h_me, c)], dst.at[my_rows], in_recv.at[c, which]
        ).start()

    for c in range(CHUNKS):
        send_in(c, 0, k_in, kv.at[c, 0, 0])
        send_in(c, 0, v_in, kv.at[c, 1, 0])

    lane_slot = lax.rem(lax.broadcasted_iota(jnp.int32, (8, 128), 1) // PIECE, 2)
    first = jnp.where(chosen_ref[0, 1] != c_me, chosen_ref[0, 1], -1)
    second = jnp.where(chosen_ref[0, 2] != c_me, chosen_ref[0, 2], -1)
    my_list[...] = jnp.where(lane_slot == 0, first, second)
    ctx_peers(
        lambda p: remote(my_list, lists.at[c_me], list_send, list_recv, p, h_me).start()
    )
    pltpu.make_async_copy(my_list, lists.at[c_me], list_recv).start()

    for c in range(CHUNKS):
        send_in(c, 1, q_in, qg.at[c, 0])
        send_in(c, 1, g_in, qg.at[c, 1])

    for c in range(CHUNKS):
        await_bytes(kv.at[c, :, 0], in_recv.at[c, 0])
        ctx_peers(
            lambda p: remote(
                kv.at[c, :, 0, piece_rows(p)],
                table.at[c, :, c_me],
                piece_send.at[c],
                piece_recv.at[c],
                p,
                h_me,
            ).start()
        )
        pltpu.make_async_copy(
            kv.at[c, :, 0, piece_rows(c_me)], table.at[c, :, c_me], piece_recv.at[c]
        ).start()
        remote(
            kv.at[c, :, 0], kv.at[c, :, 1], prev_send.at[c], prev_recv.at[c], next_ctx, h_me
        ).start()

    await_bytes(lists, list_recv)
    items = 2 * nctx * PIECE
    keys_total = nctx * PIECE
    width = min(128, items)
    per = width // (2 * PIECE)
    for t in range(items // width):
        lane_owner = lax.broadcasted_iota(jnp.int32, (8, 128), 1) // (2 * PIECE)
        target = lists[t * per]
        for i in range(1, per):
            target = jnp.where(lane_owner == i, lists[t * per + i], target)
        row = lax.broadcasted_iota(jnp.int32, (keys_total, 128), 0)
        lane = lax.broadcasted_iota(jnp.int32, (keys_total, 128), 1)
        hit = (row // PIECE == target[0:1, :]) & (lax.rem(row, PIECE) == lax.rem(lane, PIECE))
        unpick[:, t * width : (t + 1) * width] = jnp.where(hit, 1.0, 0.0).astype(jnp.bfloat16)
        flat = jnp.broadcast_to(target[0:1, :], (128, 128)).astype(jnp.float32).T
        flat = flat.astype(jnp.int32)
        for u in range(max(1, keys_total // 128)):
            wide = min(128, keys_total)
            row = lax.broadcasted_iota(jnp.int32, (128, 128), 0)
            lane = lax.broadcasted_iota(jnp.int32, (128, 128), 1)
            hit = (lane // PIECE + u * (128 // PIECE) == flat) & (
                lax.rem(row, PIECE) == lax.rem(lane, PIECE)
            )
            pick[t * width : (t + 1) * width, u * wide : (u + 1) * wide] = jnp.where(
                hit, 1.0, 0.0
            ).astype(jnp.bfloat16)[:, :wide]

    for c in range(CHUNKS):
        await_bytes(table.at[c], piece_recv.at[c])
        for which in range(2):
            found = mm(pick[...], table[c, which].reshape(keys_total, lanes), ((1,), (0,)))
            staging[c, :, which] = found.astype(jnp.bfloat16).reshape(nctx, 2, PIECE, lanes)
        ctx_peers(
            lambda p: remote(
                staging.at[c, p],
                kv.at[c, :, pl.ds(2, 2), piece_rows(c_me)],
                far_send.at[c],
                far_recv.at[c],
                p,
                h_me,
            ).start()
        )
        pltpu.make_async_copy(
            staging.at[c, c_me], kv.at[c, :, pl.ds(2, 2), piece_rows(c_me)], far_recv.at[c]
        ).start()

    half = BLOCK // 2
    used = [jnp.where(chosen_ref[0, s] != c_me, -(2**20), 2**20) for s in range(TOPK)]

    def tile_offset(t):
        blk = t // 2
        off = jnp.where(blk == 0, t * half, used[2])
        off = jnp.where(blk == 1, used[0], off)
        return jnp.where(blk == 2, used[1], off)

    def folded(x, op):
        return op(x.reshape(half // 8, 8, BLOCK), axis=0)

    for c in range(CHUNKS):
        await_bytes(qg.at[c], in_recv.at[c, 1])
        await_bytes(kv.at[c, :, 1], prev_recv.at[c])
        await_bytes(kv.at[c, :, pl.ds(2, 2)], far_recv.at[c])

        def per_head(n, carry, c=c):
            cols = pl.ds(pl.multiple_of(n * HD, HD), HD)
            q = qg[c, 0, :, cols]
            g = qg[c, 1, :, cols]

            def tile_rows(t):
                return pl.ds(pl.multiple_of(lax.rem(t, 2) * half, half), half)

            def find_scores(t, largest):
                keys = kv[c, 0, t // 2, tile_rows(t), cols]
                s = mm(keys, q, ((1,), (1,)))
                key_at = lax.broadcasted_iota(jnp.int32, (half, BLOCK), 0) + tile_offset(t)
                query_at = lax.broadcasted_iota(jnp.int32, (half, BLOCK), 1)
                s = jnp.where(key_at <= query_at, s, masked_score)
                score_scr[t] = s
                return jnp.maximum(largest, folded(s, jnp.max))

            largest = lax.fori_loop(
                0, 8, find_scores, jnp.full((8, BLOCK), masked_score, jnp.float32)
            )
            largest = jnp.max(largest, axis=0, keepdims=True)

            def find_totals(t, totals):
                values = kv[c, 1, t // 2, tile_rows(t), cols]
                d = mm(values, g, ((1,), (1,)))
                e = jnp.exp2((score_scr[t] - largest) * factor)
                score_scr[t] = e
                dprob_scr[t] = d
                return totals[0] + folded(e, jnp.sum), totals[1] + folded(e * d, jnp.sum)

            zero = jnp.zeros((8, BLOCK), jnp.float32)
            total, total_d = lax.fori_loop(0, 8, find_totals, (zero, zero))
            inverse = 1.0 / jnp.sum(total, axis=0, keepdims=True)
            delta = jnp.sum(total_d, axis=0, keepdims=True) * inverse

            def find_grads(t, dq):
                keys = kv[c, 0, t // 2, tile_rows(t), cols]
                p = score_scr[t] * inverse
                ds = (p * (dprob_scr[t] - delta)).astype(jnp.bfloat16)
                dv = mm(p.astype(jnp.bfloat16), g, ((1,), (0,)))
                dk = mm(ds, q, ((1,), (0,))) * scaling
                return dk, dv, dq + mm(keys, ds, ((0,), (0,)))

            def own_tile(t, dq):
                dk, dv, dq = find_grads(t, dq)
                own_grad[c, 0, tile_rows(t), cols] = dk
                own_grad[c, 1, tile_rows(t), cols] = dv
                return dq

            def far_tile(t, dq):
                dk, dv, dq = find_grads(t, dq)
                far_grad[c, 0, t // 2 - 1, tile_rows(t), cols] = dk.astype(jnp.bfloat16)
                far_grad[c, 1, t // 2 - 1, tile_rows(t), cols] = dv.astype(jnp.bfloat16)
                return dq

            dq = lax.fori_loop(0, 2, own_tile, jnp.zeros((HD, BLOCK), jnp.float32))
            dq = lax.fori_loop(2, 8, far_tile, dq)
            done[c, 0, :, cols] = (dq.T * scaling).astype(jnp.bfloat16)
            return carry

        lax.fori_loop(0, heads, per_head, 0)

        ctx_peers(
            lambda p: remote(
                far_grad.at[c, :, pl.ds(1, 2), piece_rows(p)],
                parts.at[c, :, c_me],
                grad_send.at[c],
                grad_recv.at[c],
                p,
                h_me,
            ).start()
        )
        pltpu.make_async_copy(
            far_grad.at[c, :, pl.ds(1, 2), piece_rows(c_me)], parts.at[c, :, c_me], grad_recv.at[c]
        ).start()
        remote(
            far_grad.at[c, :, 0], prev_back.at[c], pgrad_send.at[c], pgrad_recv.at[c], last_ctx, h_me
        ).start()

    def slab_rows(peer):
        return pl.ds(pl.multiple_of(peer * rows, rows), rows)

    def send_out(c, which, dst):
        head_peers(
            lambda p: remote(
                done.at[c, which, slab_rows(p)],
                dst.at[:, slab_columns(h_me, c)],
                out_send.at[which],
                out_recv.at[which],
                c_me,
                p,
            ).start()
        )
        pltpu.make_async_copy(
            done.at[c, which, my_rows], dst.at[:, slab_columns(h_me, c)], out_recv.at[which]
        ).start()

    for c in range(CHUNKS):
        await_bytes(parts.at[c], grad_recv.at[c])
        for which in range(2):
            total = mm(unpick[...], parts[c, which].reshape(items, lanes), ((1,), (0,)))
            sums[c, :, which] = total.astype(jnp.bfloat16).reshape(nctx, PIECE, lanes)
        ctx_peers(
            lambda p: remote(
                sums.at[c, p],
                back.at[c, :, piece_rows(c_me)],
                sum_send.at[c],
                sum_recv.at[c],
                p,
                h_me,
            ).start()
        )
        pltpu.make_async_copy(
            sums.at[c, c_me], back.at[c, :, piece_rows(c_me)], sum_recv.at[c]
        ).start()
        send_out(c, 0, q_out)

    for c in range(CHUNKS):
        await_bytes(prev_back.at[c], pgrad_recv.at[c])
        await_bytes(back.at[c], sum_recv.at[c])
        for which in range(2):
            total = own_grad[c, which] + prev_back[c, which].astype(jnp.float32)
            total = total + back[c, which].astype(jnp.float32)
            done[c, 1 + which] = total.astype(jnp.bfloat16)
        send_out(c, 1, k_out)
        send_out(c, 2, v_out)

    others = pl.ds(0, nctx - 1)
    other_rows = pl.ds(0, (nctx - 1) * PIECE)
    slab_others = pl.ds(0, (nhead - 1) * rows)
    await_bytes(lists.at[others], list_send)
    for c in range(CHUNKS):
        await_bytes(kv.at[c, :, 0, slab_others], in_send.at[c, 0])
        await_bytes(qg.at[c, :, slab_others], in_send.at[c, 1])
        await_bytes(kv.at[c, :, 0, other_rows], piece_send.at[c])
        await_bytes(kv.at[c, :, 0], prev_send.at[c])
        await_bytes(staging.at[c, others], far_send.at[c])
        await_bytes(far_grad.at[c, :, pl.ds(1, 2), other_rows], grad_send.at[c])
        await_bytes(far_grad.at[c, :, 0], pgrad_send.at[c])
        await_bytes(sums.at[c, others], sum_send.at[c])
    for which, out in enumerate((q_out, k_out, v_out)):
        await_bytes(done.at[:, which, slab_others], out_send.at[which])
        await_bytes(out, out_recv.at[which])


def per_device(queries, key_vectors, value_vectors, out_grad, chosen):
    nctx = lax.axis_size("ctx")
    nhead = lax.axis_size("head")
    lanes = H * HD // nhead // CHUNKS
    n = CHUNKS
    bf = jnp.bfloat16
    f32 = jnp.float32
    dma = pltpu.SemaphoreType.DMA
    anywhere = pl.BlockSpec(memory_space=pl.ANY)
    slab = jax.ShapeDtypeStruct(queries.shape, bf)
    scratch = [
        pltpu.VMEM((n, 2, 4, BLOCK, lanes), bf),
        pltpu.VMEM((n, 2, BLOCK, lanes), bf),
        pltpu.VMEM((n, 2, nctx, PIECE, lanes), bf),
        pltpu.VMEM((n, nctx, 2, 2, PIECE, lanes), bf),
        pltpu.VMEM((n, 2, 3, BLOCK, lanes), bf),
        pltpu.VMEM((n, 2, BLOCK, lanes), f32),
        pltpu.VMEM((n, 2, nctx, 2, PIECE, lanes), bf),
        pltpu.VMEM((n, nctx, 2, PIECE, lanes), bf),
        pltpu.VMEM((n, 2, BLOCK, lanes), bf),
        pltpu.VMEM((n, 2, BLOCK, lanes), bf),
        pltpu.VMEM((n, 3, BLOCK, lanes), bf),
        pltpu.VMEM((2 * nctx * PIECE, nctx * PIECE), bf),
        pltpu.VMEM((nctx * PIECE, 2 * nctx * PIECE), bf),
        pltpu.VMEM((8, BLOCK // 2, BLOCK), f32),
        pltpu.VMEM((8, BLOCK // 2, BLOCK), f32),
        pltpu.VMEM((8, 128), jnp.int32),
        pltpu.VMEM((nctx, 8, 128), jnp.int32),
        dma,
        dma,
        dma((n, 2)),
        dma((n, 2)),
    ]
    scratch += [dma((n,)) for _ in range(12)]
    scratch += [dma((3,)), dma((3,))]
    return pl.pallas_call(
        functools.partial(kernel, nctx, nhead),
        out_shape=(slab, slab, slab),
        in_specs=[anywhere] * 4 + [pl.BlockSpec(memory_space=pltpu.SMEM)],
        out_specs=(anywhere,) * 3,
        scratch_shapes=scratch,
        compiler_params=pltpu.CompilerParams(
            collective_id=0, has_side_effects=True, vmem_limit_bytes=60 * 2**20
        ),
        name="sparse_attention_backward",
    )(queries, key_vectors, value_vectors, out_grad, chosen)


def solution(mesh):
    slabs = P(("ctx", "head"), None)
    return jax.shard_map(
        per_device,
        mesh=mesh,
        in_specs=(slabs, slabs, slabs, slabs, P("ctx", None)),
        out_specs=(slabs, slabs, slabs),
        check_vma=False,
    )
```

```python
import functools

import jax
import jax.numpy as jnp
from jax import lax
from jax.experimental import pallas as pl
from jax.experimental.pallas import tpu as pltpu
from jax.sharding import PartitionSpec as P

H = 64
HD = 128
BLOCK = 512
TOPK = 3
RING = 4
PIECE = 16
MESH = pl.DeviceIdType.MESH
LOG2E = 1.4426950408889634
masked_score = -1e30
KEY, VALUE = 0, 1
QUERY, GRAD = 0, 1


def mm(a, b, dims):
    return lax.dot_general(a, b, (dims, ((), ())), preferred_element_type=jnp.float32)


def kernel(
    levels,
    nhead,
    q_in,
    k_in,
    v_in,
    g_in,
    chosen_ref,
    q_out,
    k_out,
    v_out,
    keys,
    values,
    qg,
    weights,
    scratch,
    pairs,
    own,
    partial,
    halves,
    parts,
    done,
    choose,
    my_list,
    lists,
    targets,
    list_send,
    list_recv,
    list_local,
    in_send,
    in_recv,
    ring_send,
    ring_recv,
    part_send,
    part_recv,
    out_send,
    out_recv,
):
    c_me = lax.axis_index("ctx")
    h_me = lax.axis_index("head")
    z_me = c_me // RING
    x_me = lax.rem(c_me, RING)
    rows = BLOCK // nhead
    column_chunks = nhead // 2
    chunk = BLOCK // column_chunks
    half = BLOCK // 2
    scaling = HD ** (-0.5)
    factor = scaling * LOG2E
    group = levels * nhead

    def remote(src, dst, send, recv, z_to, x_to, h_to):
        return pltpu.make_async_remote_copy(
            src_ref=src,
            dst_ref=dst,
            send_sem=send,
            recv_sem=recv,
            device_id=(z_to * RING + x_to, h_to),
            device_id_type=MESH,
        )

    def await_bytes(ref, sem):
        pltpu.make_async_copy(ref, ref, sem).wait()

    def group_peers(body):
        def step(k, carry):
            body(lax.rem(z_me + lax.rem(k, levels), levels), lax.rem(h_me + k // levels, nhead))
            return carry

        lax.fori_loop(1, group, step, 0)

    def signal(z_to, x_to, h_to):
        pl.semaphore_signal(
            barrier, inc=1, device_id=(z_to * RING + x_to, h_to), device_id_type=MESH
        )

    barrier = pltpu.get_barrier_semaphore()
    group_peers(lambda z, h: signal(z, x_me, h))
    for x in (lax.rem(x_me + 1, RING), lax.rem(x_me + RING - 1, RING)):
        signal(z_me, x, h_me)
    pl.semaphore_wait(barrier, group + 1)

    def head_columns(z, h):
        return pl.ds(pl.multiple_of((z * nhead + h) * HD, HD), HD)

    def slab_rows(h):
        return pl.ds(pl.multiple_of(h * rows, rows), rows)

    def send_in(which, src, dst):
        group_peers(
            lambda z, h: remote(
                src.at[:, head_columns(z, h)],
                dst.at[z_me, slab_rows(h_me)],
                in_send.at[which],
                in_recv.at[which],
                z,
                x_me,
                h,
            ).start()
        )
        pltpu.make_async_copy(
            src.at[:, head_columns(z_me, h_me)], dst.at[z_me, slab_rows(h_me)], in_recv.at[which]
        ).start()

    send_in(0, k_in, keys.at[x_me])

    lane = lax.broadcasted_iota(jnp.int32, (8, 128), 1)
    my_list[...] = jnp.where(
        lane == 0, chosen_ref[0, 0], jnp.where(lane == 1, chosen_ref[0, 1], chosen_ref[0, 2])
    )

    def send_list(k, carry):
        remote(
            my_list, lists.at[z_me], list_send, list_recv, lax.rem(z_me + k, levels), x_me, h_me
        ).start()
        return carry

    lax.fori_loop(1, levels, send_list, 0)
    pltpu.make_async_copy(my_list, lists.at[z_me], list_recv).start()

    send_in(1, q_in, qg.at[QUERY])
    send_in(2, v_in, values.at[x_me])
    send_in(3, g_in, qg.at[GRAD])

    await_bytes(lists, list_recv)
    to_scalars = pltpu.make_async_copy(lists, targets, list_local)
    to_scalars.start()
    to_scalars.wait()

    span = levels * PIECE
    for s in range(TOPK):
        lane = lax.broadcasted_iota(jnp.int32, (RING * span, span), 1)
        row = lax.broadcasted_iota(jnp.int32, (RING * span, span), 0)
        target = jnp.full((RING * span, span), -1, jnp.int32)
        for z in range(levels):
            target = jnp.where(lane // PIECE == z, targets[z, 0, s], target)
        block = lax.rem(row // PIECE, levels) * RING + row // span
        hit = (block == target) & (lax.rem(row, PIECE) == lax.rem(lane, PIECE))
        choose[:, s * span : (s + 1) * span] = jnp.where(hit, 1.0, 0.0).astype(jnp.bfloat16)

    right = lax.rem(x_me + 1, RING)
    left = lax.rem(x_me + RING - 1, RING)
    low = pl.ds(0, levels // 2)
    high = pl.ds(levels // 2, levels // 2)

    def ring_copy(src, dst, sems, to):
        return remote(src, dst, sems[0], sems[1], z_me, to, h_me)

    def share(which, arrived, blocks):
        await_bytes(blocks.at[x_me], in_recv.at[arrived])
        for side, to in enumerate((right, left)):
            ring_copy(
                blocks.at[x_me],
                blocks.at[x_me],
                (ring_send.at[which, side], ring_recv.at[which, side]),
                to,
            ).start()

    def pass_on(which, blocks):
        for side, (source, part, to) in enumerate(((left, low, right), (right, high, left))):
            await_bytes(blocks.at[source], ring_recv.at[which, side])
            ring_copy(
                blocks.at[source, part],
                blocks.at[source, part],
                (ring_send.at[which, 2 + side], ring_recv.at[which, 2 + side]),
                to,
            ).start()

    def await_shared(which, blocks):
        for side, part in enumerate((low, high)):
            await_bytes(blocks.at[0, part], ring_recv.at[which, 2 + side])

    def tile_rows(t):
        return pl.ds(pl.multiple_of(lax.rem(t, 2) * half, half), half)

    def tile_block(z, t):
        mine = z * RING + x_me
        block = jnp.where(t < 2, mine, targets[z, 0, jnp.maximum(t // 2 - 1, 0)])
        far = jnp.where(block != mine, -(2**20), 2**20)
        return lax.rem(block, RING), block // RING, jnp.where(t < 2, t * half, far)

    def folded(x, op):
        return op(x.reshape(half // 8, 8, BLOCK), axis=0)

    def level_loop(body, start=0, stop=levels):
        def step(k, carry):
            body(lax.rem(z_me + k, levels))
            return carry

        lax.fori_loop(start, stop, step, 0)

    share(KEY, 0, keys)
    pass_on(KEY, keys)
    await_bytes(qg.at[QUERY], in_recv.at[1])
    await_shared(KEY, keys)

    def find_weights(z):
        q = qg[QUERY, z]

        def find_scores(t, largest):
            xb, zb, offset = tile_block(z, t)
            s = mm(keys[xb, zb, tile_rows(t)], q, ((1,), (1,)))
            key_at = lax.broadcasted_iota(jnp.int32, (half, BLOCK), 0) + offset
            query_at = lax.broadcasted_iota(jnp.int32, (half, BLOCK), 1)
            s = jnp.where(key_at <= query_at, s, masked_score)
            scratch[t] = s
            return jnp.maximum(largest, folded(s, jnp.max))

        largest = lax.fori_loop(
            0, 8, find_scores, jnp.full((8, BLOCK), masked_score, jnp.float32)
        )
        largest = jnp.max(largest, axis=0, keepdims=True)

        def find_total(t, total):
            e = jnp.exp2((scratch[t] - largest) * factor)
            scratch[t] = e
            return total + folded(e, jnp.sum)

        total = lax.fori_loop(0, 8, find_total, jnp.zeros((8, BLOCK), jnp.float32))
        inverse = 1.0 / jnp.sum(total, axis=0, keepdims=True)

        def divide(t, carry):
            weights[z, t] = (scratch[t] * inverse).astype(jnp.bfloat16)
            return carry

        lax.fori_loop(0, 8, divide, 0)

    level_loop(find_weights, 0, levels // 2)
    share(VALUE, 2, values)
    level_loop(find_weights, levels // 2, levels)

    pass_on(VALUE, values)
    await_bytes(qg.at[GRAD], in_recv.at[3])

    def find_value_terms(z):
        g = qg[GRAD, z]

        def own_tile(t, carry):
            own[VALUE, z, tile_rows(t)] = mm(weights[z, t], g, ((1,), (0,)))
            return carry

        def far_tile(t, carry):
            term = mm(weights[z, t], g, ((1,), (0,)))
            pairs[VALUE, t // 2 - 1, z, tile_rows(t)] = term.astype(jnp.bfloat16)
            return carry

        lax.fori_loop(0, 2, own_tile, 0)
        lax.fori_loop(2, 8, far_tile, 0)

    level_loop(find_value_terms)

    y_me = h_me // 2

    across = lax.rem(x_me + 2, RING)

    def chunk_start(i):
        return lax.rem(y_me + i, column_chunks) * chunk

    def chunk_rows(i):
        return pl.ds(pl.multiple_of(chunk_start(i), chunk), chunk)

    def send_terms(which):
        for i in range(column_chunks):

            def add_rows(n, carry, i=i):
                at = pl.ds(pl.multiple_of(chunk_start(i) + n * PIECE, PIECE), PIECE)
                terms = pairs[which, :, :, at].reshape(TOPK * span, HD)
                total = mm(choose[...], terms, ((1,), (0,)))
                partial[which, :, :, at] = total.astype(jnp.bfloat16).reshape(
                    RING, levels, PIECE, HD
                )
                return carry

            lax.fori_loop(0, chunk // PIECE, add_rows, 0)
            at = chunk_rows(i)
            for side, (part, to) in enumerate(((low, right), (high, left))):
                ring_copy(
                    partial.at[which, across, part, at],
                    halves.at[which, side, :, at],
                    (part_send.at[which, side, i], part_recv.at[which, side, i]),
                    to,
                ).start()

    def send_sums(which):
        for i in range(column_chunks):
            at = chunk_rows(i)
            for side, (start, to) in enumerate(((0, right), (levels // 2, left))):
                await_bytes(halves.at[which, side, :, at], part_recv.at[which, side, i])

                def add_level(n, carry, at=at, side=side, start=start, to=to):
                    both = partial[which, to, start + n, at].astype(jnp.float32)
                    both = both + halves[which, side, n, at].astype(jnp.float32)
                    partial[which, to, start + n, at] = both.astype(jnp.bfloat16)
                    return carry

                lax.fori_loop(0, levels // 2, add_level, 0)
                ring_copy(
                    partial.at[which, to, :, at],
                    parts.at[which, side, :, at],
                    (part_send.at[which, 2 + side, i], part_recv.at[which, 2 + side, i]),
                    to,
                ).start()

    def send_out(which, z, h, dst):
        here = done.at[which, z, slab_rows(h)]
        there = dst.at[:, head_columns(z_me, h_me)]
        mine = (z == z_me) & (h == h_me)

        @pl.when(mine)
        def _():
            pltpu.make_async_copy(here, there, out_recv.at[which]).start()

        @pl.when(jnp.logical_not(mine))
        def _():
            remote(here, there, out_send.at[which], out_recv.at[which], z, x_me, h).start()

    def finish(which, dst):
        for i in range(column_chunks):
            at = chunk_rows(i)
            for side in range(2):
                await_bytes(parts.at[which, side, :, at], part_recv.at[which, 2 + side, i])

            def add_level(z, at=at):
                total = own[which, z, at] + partial[which, x_me, z, at].astype(jnp.float32)
                for side in range(2):
                    total = total + parts[which, side, z, at].astype(jnp.float32)
                done[1 + which, z, at] = total.astype(jnp.bfloat16)

            level_loop(add_level)

            def send_level(z, i=i):
                for n in range(2):
                    send_out(1 + which, z, lax.rem(y_me + i, column_chunks) * 2 + n, dst)

            level_loop(send_level)

    send_terms(VALUE)

    await_shared(VALUE, values)

    def find_key_terms(z):
        q = qg[QUERY, z]
        g = qg[GRAD, z]

        def find_dprobs(t, delta):
            xb, zb, offset = tile_block(z, t)
            d = mm(values[xb, zb, tile_rows(t)], g, ((1,), (1,)))
            scratch[t] = d
            return delta + folded(weights[z, t].astype(jnp.float32) * d, jnp.sum)

        delta = lax.fori_loop(0, 8, find_dprobs, jnp.zeros((8, BLOCK), jnp.float32))
        delta = jnp.sum(delta, axis=0, keepdims=True)

        def find_terms(t, dq):
            xb, zb, offset = tile_block(z, t)
            key_rows = keys[xb, zb, tile_rows(t)]
            ds = (weights[z, t].astype(jnp.float32) * (scratch[t] - delta)).astype(jnp.bfloat16)
            return mm(ds, q, ((1,), (0,))) * scaling, dq + mm(key_rows, ds, ((0,), (0,)))

        def own_tile(t, dq):
            dk, dq = find_terms(t, dq)
            own[KEY, z, tile_rows(t)] = dk
            return dq

        def far_tile(t, dq):
            dk, dq = find_terms(t, dq)
            pairs[KEY, t // 2 - 1, z, tile_rows(t)] = dk.astype(jnp.bfloat16)
            return dq

        dq = lax.fori_loop(0, 2, own_tile, jnp.zeros((HD, BLOCK), jnp.float32))
        dq = lax.fori_loop(2, 8, far_tile, dq)
        done[0, z] = (dq.T * scaling).astype(jnp.bfloat16)

        def send_rows(k, carry):
            send_out(0, z, lax.rem(h_me + k, nhead), q_out)
            return carry

        lax.fori_loop(0, nhead, send_rows, 0)

    level_loop(find_key_terms, 0, levels // 2)
    send_sums(VALUE)
    level_loop(find_key_terms, levels // 2, levels)
    send_terms(KEY)
    send_sums(KEY)
    finish(VALUE, v_out)
    finish(KEY, k_out)

    others_columns = pl.ds(0, (group - 1) * HD)
    await_bytes(lists.at[pl.ds(0, levels - 1)], list_send)
    for which, src in enumerate((k_in, q_in, v_in, g_in)):
        await_bytes(src.at[:, others_columns], in_send.at[which])
    for which in range(2):
        for side in range(2):
            await_bytes(keys.at[0], ring_send.at[which, side])
            await_bytes(keys.at[0, low], ring_send.at[which, 2 + side])
            for i in range(column_chunks):
                at = pl.ds(0, chunk)
                await_bytes(halves.at[which, side, :, at], part_send.at[which, side, i])
                await_bytes(parts.at[which, side, :, at], part_send.at[which, 2 + side, i])
    for which, out in enumerate((q_out, k_out, v_out)):
        await_bytes(out.at[:, others_columns], out_send.at[which])
        await_bytes(out, out_recv.at[which])


def per_device(queries, key_vectors, value_vectors, out_grad, chosen):
    levels = lax.axis_size("ctx") // RING
    nhead = lax.axis_size("head")
    bf = jnp.bfloat16
    f32 = jnp.float32
    dma = pltpu.SemaphoreType.DMA
    anywhere = pl.BlockSpec(memory_space=pl.ANY)
    slab = jax.ShapeDtypeStruct(queries.shape, bf)
    span = levels * PIECE
    scratch = [
        pltpu.VMEM((RING, levels, BLOCK, HD), bf),
        pltpu.VMEM((RING, levels, BLOCK, HD), bf),
        pltpu.VMEM((2, levels, BLOCK, HD), bf),
        pltpu.VMEM((levels, 8, BLOCK // 2, BLOCK), bf),
        pltpu.VMEM((8, BLOCK // 2, BLOCK), f32),
        pltpu.VMEM((2, TOPK, levels, BLOCK, HD), bf),
        pltpu.VMEM((2, levels, BLOCK, HD), f32),
        pltpu.VMEM((2, RING, levels, BLOCK, HD), bf),
        pltpu.VMEM((2, 2, levels // 2, BLOCK, HD), bf),
        pltpu.VMEM((2, 2, levels, BLOCK, HD), bf),
        pltpu.VMEM((3, levels, BLOCK, HD), bf),
        pltpu.VMEM((RING * span, TOPK * span), bf),
        pltpu.VMEM((8, 128), jnp.int32),
        pltpu.VMEM((levels, 8, 128), jnp.int32),
        pltpu.SMEM((levels, 8, 128), jnp.int32),
        dma,
        dma,
        dma,
        dma((4,)),
        dma((4,)),
        dma((2, 4)),
        dma((2, 4)),
        dma((2, 4, nhead // 2)),
        dma((2, 4, nhead // 2)),
        dma((3,)),
        dma((3,)),
    ]
    return pl.pallas_call(
        functools.partial(kernel, levels, nhead),
        out_shape=(slab, slab, slab),
        in_specs=[anywhere] * 4 + [pl.BlockSpec(memory_space=pltpu.SMEM)],
        out_specs=(anywhere,) * 3,
        scratch_shapes=scratch,
        compiler_params=pltpu.CompilerParams(
            collective_id=0, has_side_effects=True, vmem_limit_bytes=62 * 2**20
        ),
        name="sparse_attention_backward",
    )(queries, key_vectors, value_vectors, out_grad, chosen)


def solution(mesh):
    slabs = P(("ctx", "head"), None)
    return jax.shard_map(
        per_device,
        mesh=mesh,
        in_specs=(slabs, slabs, slabs, slabs, P("ctx", None)),
        out_specs=(slabs, slabs, slabs),
        check_vma=False,
    )
```

```python
import functools

import jax
import jax.numpy as jnp
from jax import lax
from jax.experimental import pallas as pl
from jax.experimental.pallas import tpu as pltpu
from jax.sharding import PartitionSpec as P

H = 64
HD = 128
BLOCK = 512
TOPK = 3
RING = 4
PIECE = 16
MESH = pl.DeviceIdType.MESH
LOG2E = 1.4426950408889634
masked_score = -1e30
KEY, VALUE = 0, 1
QUERY, GRAD = 0, 1


def mm(a, b, dims):
    return lax.dot_general(a, b, (dims, ((), ())), preferred_element_type=jnp.float32)


def kernel(
    levels,
    nhead,
    q_in,
    k_in,
    v_in,
    g_in,
    chosen_ref,
    q_out,
    k_out,
    v_out,
    keys,
    values,
    qg,
    weights,
    scratch,
    pairs,
    own,
    partial,
    halves,
    parts,
    done,
    choose,
    my_list,
    lists,
    targets,
    list_send,
    list_recv,
    list_local,
    in_send,
    in_recv,
    ring_send,
    ring_recv,
    part_send,
    part_recv,
    out_send,
    out_recv,
):
    c_me = lax.axis_index("ctx")
    h_me = lax.axis_index("head")
    z_me = c_me // RING
    x_me = lax.rem(c_me, RING)
    rows = BLOCK // nhead
    column_chunks = nhead // 2
    chunk = BLOCK // column_chunks
    half = BLOCK // 2
    scaling = HD ** (-0.5)
    factor = scaling * LOG2E
    group = levels * nhead

    def remote(src, dst, send, recv, z_to, x_to, h_to):
        return pltpu.make_async_remote_copy(
            src_ref=src,
            dst_ref=dst,
            send_sem=send,
            recv_sem=recv,
            device_id=(z_to * RING + x_to, h_to),
            device_id_type=MESH,
        )

    def await_bytes(ref, sem):
        pltpu.make_async_copy(ref, ref, sem).wait()

    def near_level(k):
        step = jnp.where(lax.rem(k, 2) == 1, (k + 1) // 2, levels - k // 2)
        return lax.rem(z_me + step, levels)

    def group_peers(body):
        def step(k, carry):
            body(lax.rem(z_me + lax.rem(k, levels), levels), lax.rem(h_me + k // levels, nhead))
            return carry

        lax.fori_loop(1, group, step, 0)

    def near_peers_first(body):
        def step(k, carry):
            body(near_level(k // nhead), lax.rem(h_me + lax.rem(k, nhead), nhead))
            return carry

        lax.fori_loop(1, group, step, 0)

    def signal(z_to, x_to, h_to):
        pl.semaphore_signal(
            barrier, inc=1, device_id=(z_to * RING + x_to, h_to), device_id_type=MESH
        )

    barrier = pltpu.get_barrier_semaphore()
    group_peers(lambda z, h: signal(z, x_me, h))
    for x in (lax.rem(x_me + 1, RING), lax.rem(x_me + RING - 1, RING)):
        signal(z_me, x, h_me)
    pl.semaphore_wait(barrier, group + 1)

    def head_columns(z, h):
        return pl.ds(pl.multiple_of((z * nhead + h) * HD, HD), HD)

    def slab_rows(h):
        return pl.ds(pl.multiple_of(h * rows, rows), rows)

    def send_in(which, src, dst, peers):
        peers(
            lambda z, h: remote(
                src.at[:, head_columns(z, h)],
                dst.at[z_me, slab_rows(h_me)],
                in_send.at[which],
                in_recv.at[which, z_me],
                z,
                x_me,
                h,
            ).start()
        )
        pltpu.make_async_copy(
            src.at[:, head_columns(z_me, h_me)],
            dst.at[z_me, slab_rows(h_me)],
            in_recv.at[which, z_me],
        ).start()

    send_in(0, k_in, keys.at[x_me], group_peers)

    lane = lax.broadcasted_iota(jnp.int32, (8, 128), 1)
    my_list[...] = jnp.where(
        lane == 0, chosen_ref[0, 0], jnp.where(lane == 1, chosen_ref[0, 1], chosen_ref[0, 2])
    )

    def send_list(k, carry):
        remote(
            my_list, lists.at[z_me], list_send, list_recv, lax.rem(z_me + k, levels), x_me, h_me
        ).start()
        return carry

    lax.fori_loop(1, levels, send_list, 0)
    pltpu.make_async_copy(my_list, lists.at[z_me], list_recv).start()

    send_in(1, v_in, values.at[x_me], group_peers)
    send_in(2, q_in, qg.at[QUERY], near_peers_first)
    send_in(3, g_in, qg.at[GRAD], near_peers_first)

    await_bytes(lists, list_recv)
    to_scalars = pltpu.make_async_copy(lists, targets, list_local)
    to_scalars.start()
    to_scalars.wait()

    span = levels * PIECE
    for s in range(TOPK):
        lane = lax.broadcasted_iota(jnp.int32, (RING * span, span), 1)
        row = lax.broadcasted_iota(jnp.int32, (RING * span, span), 0)
        target = jnp.full((RING * span, span), -1, jnp.int32)
        for z in range(levels):
            target = jnp.where(lane // PIECE == z, targets[z, 0, s], target)
        block = lax.rem(row // PIECE, levels) * RING + row // span
        hit = (block == target) & (lax.rem(row, PIECE) == lax.rem(lane, PIECE))
        choose[:, s * span : (s + 1) * span] = jnp.where(hit, 1.0, 0.0).astype(jnp.bfloat16)

    right = lax.rem(x_me + 1, RING)
    left = lax.rem(x_me + RING - 1, RING)
    low = pl.ds(0, levels // 2)
    high = pl.ds(levels // 2, levels // 2)

    def ring_copy(src, dst, sems, to):
        return remote(src, dst, sems[0], sems[1], z_me, to, h_me)

    def share(which, blocks):
        def await_level(z, carry):
            await_bytes(blocks.at[x_me, z], in_recv.at[which, z])
            return carry

        lax.fori_loop(0, levels, await_level, 0)
        for side, to in enumerate((right, left)):
            ring_copy(
                blocks.at[x_me],
                blocks.at[x_me],
                (ring_send.at[which, side], ring_recv.at[which, side]),
                to,
            ).start()

    def pass_on(which, blocks):
        for side, (source, part, to) in enumerate(((left, low, right), (right, high, left))):
            await_bytes(blocks.at[source], ring_recv.at[which, side])
            ring_copy(
                blocks.at[source, part],
                blocks.at[source, part],
                (ring_send.at[which, 2 + side], ring_recv.at[which, 2 + side]),
                to,
            ).start()

    def await_shared(which, blocks):
        for side, part in enumerate((low, high)):
            await_bytes(blocks.at[0, part], ring_recv.at[which, 2 + side])

    def tile_rows(t):
        return pl.ds(pl.multiple_of(lax.rem(t, 2) * half, half), half)

    def tile_block(z, t):
        mine = z * RING + x_me
        block = jnp.where(t < 2, mine, targets[z, 0, jnp.maximum(t // 2 - 1, 0)])
        far = jnp.where(block != mine, -(2**20), 2**20)
        return lax.rem(block, RING), block // RING, jnp.where(t < 2, t * half, far)

    def folded(x, op):
        return op(x.reshape(half // 8, 8, BLOCK), axis=0)

    def level_loop(body, start=0, stop=levels):
        def step(k, carry):
            body(near_level(k))
            return carry

        lax.fori_loop(start, stop, step, 0)

    share(KEY, keys)
    pass_on(KEY, keys)
    share(VALUE, values)
    await_shared(KEY, keys)

    def find_weights(z):
        await_bytes(qg.at[QUERY, z], in_recv.at[2, z])
        q = qg[QUERY, z]

        def find_scores(t, largest):
            xb, zb, offset = tile_block(z, t)
            s = mm(keys[xb, zb, tile_rows(t)], q, ((1,), (1,)))
            key_at = lax.broadcasted_iota(jnp.int32, (half, BLOCK), 0) + offset
            query_at = lax.broadcasted_iota(jnp.int32, (half, BLOCK), 1)
            s = jnp.where(key_at <= query_at, s, masked_score)
            scratch[t] = s
            return jnp.maximum(largest, folded(s, jnp.max))

        largest = lax.fori_loop(
            0, 8, find_scores, jnp.full((8, BLOCK), masked_score, jnp.float32), unroll=2
        )
        largest = jnp.max(largest, axis=0, keepdims=True)

        def find_total(t, total):
            e = jnp.exp2((scratch[t] - largest) * factor)
            scratch[t] = e
            return total + folded(e, jnp.sum)

        total = lax.fori_loop(0, 8, find_total, jnp.zeros((8, BLOCK), jnp.float32), unroll=2)
        inverse = 1.0 / jnp.sum(total, axis=0, keepdims=True)

        def divide(t, carry):
            weights[z, t] = (scratch[t] * inverse).astype(jnp.bfloat16)
            return carry

        lax.fori_loop(0, 8, divide, 0, unroll=2)

    level_loop(find_weights, 0, levels // 2)
    pass_on(VALUE, values)
    level_loop(find_weights, levels // 2, levels)

    def find_value_terms(z):
        await_bytes(qg.at[GRAD, z], in_recv.at[3, z])
        g = qg[GRAD, z]

        def own_tile(t, carry):
            own[VALUE, z, tile_rows(t)] = mm(weights[z, t], g, ((1,), (0,)))
            return carry

        def far_tile(t, carry):
            term = mm(weights[z, t], g, ((1,), (0,)))
            pairs[VALUE, t // 2 - 1, z, tile_rows(t)] = term.astype(jnp.bfloat16)
            return carry

        lax.fori_loop(0, 2, own_tile, 0, unroll=2)
        lax.fori_loop(2, 8, far_tile, 0, unroll=2)

    level_loop(find_value_terms)

    y_me = h_me // 2

    across = lax.rem(x_me + 2, RING)

    def chunk_start(i):
        return lax.rem(y_me + i, column_chunks) * chunk

    def chunk_rows(i):
        return pl.ds(pl.multiple_of(chunk_start(i), chunk), chunk)

    def send_terms(which):
        for i in range(column_chunks):

            def add_rows(n, carry, i=i):
                first = chunk_start(i) + n * 2 * PIECE
                both = [
                    pl.ds(pl.multiple_of(first + m * PIECE, PIECE), PIECE) for m in range(2)
                ]
                terms = [pairs[which, :, :, at].reshape(TOPK * span, HD) for at in both]
                total = mm(choose[...], jnp.concatenate(terms, axis=1), ((1,), (0,)))
                total = total.astype(jnp.bfloat16)
                for m, at in enumerate(both):
                    partial[which, :, :, at] = total[:, m * HD : (m + 1) * HD].reshape(
                        RING, levels, PIECE, HD
                    )
                return carry

            lax.fori_loop(0, chunk // (2 * PIECE), add_rows, 0)
            at = chunk_rows(i)
            for side, (part, to) in enumerate(((low, right), (high, left))):
                ring_copy(
                    partial.at[which, across, part, at],
                    halves.at[which, side, :, at],
                    (part_send.at[which, side, i], part_recv.at[which, side, i]),
                    to,
                ).start()

    def send_sums(which):
        for i in range(column_chunks):
            at = chunk_rows(i)
            for side, (start, to) in enumerate(((0, right), (levels // 2, left))):
                await_bytes(halves.at[which, side, :, at], part_recv.at[which, side, i])

                def add_level(n, carry, at=at, side=side, start=start, to=to):
                    both = partial[which, to, start + n, at].astype(jnp.float32)
                    both = both + halves[which, side, n, at].astype(jnp.float32)
                    partial[which, to, start + n, at] = both.astype(jnp.bfloat16)
                    return carry

                lax.fori_loop(0, levels // 2, add_level, 0)
                ring_copy(
                    partial.at[which, to, :, at],
                    parts.at[which, side, :, at],
                    (part_send.at[which, 2 + side, i], part_recv.at[which, 2 + side, i]),
                    to,
                ).start()

    def send_out(which, z, h, dst):
        here = done.at[which, z, slab_rows(h)]
        there = dst.at[:, head_columns(z_me, h_me)]
        mine = (z == z_me) & (h == h_me)

        @pl.when(mine)
        def _():
            pltpu.make_async_copy(here, there, out_recv.at[which]).start()

        @pl.when(jnp.logical_not(mine))
        def _():
            remote(here, there, out_send.at[which], out_recv.at[which], z, x_me, h).start()

    def finish(which, dst):
        for i in range(column_chunks):
            at = chunk_rows(i)
            for side in range(2):
                await_bytes(parts.at[which, side, :, at], part_recv.at[which, 2 + side, i])

            def add_level(z, at=at):
                total = own[which, z, at] + partial[which, x_me, z, at].astype(jnp.float32)
                for side in range(2):
                    total = total + parts[which, side, z, at].astype(jnp.float32)
                done[1 + which, z, at] = total.astype(jnp.bfloat16)

            level_loop(add_level)

            def send_level(z, i=i):
                for n in range(2):
                    send_out(1 + which, z, lax.rem(y_me + i, column_chunks) * 2 + n, dst)

            level_loop(send_level)

    send_terms(VALUE)

    await_shared(VALUE, values)

    def find_key_terms(z):
        q = qg[QUERY, z]
        g = qg[GRAD, z]

        def find_dprobs(t, delta):
            xb, zb, offset = tile_block(z, t)
            d = mm(values[xb, zb, tile_rows(t)], g, ((1,), (1,)))
            scratch[t] = d
            return delta + folded(weights[z, t].astype(jnp.float32) * d, jnp.sum)

        delta = lax.fori_loop(0, 8, find_dprobs, jnp.zeros((8, BLOCK), jnp.float32), unroll=2)
        delta = jnp.sum(delta, axis=0, keepdims=True)

        def find_terms(t, dq):
            xb, zb, offset = tile_block(z, t)
            key_rows = keys[xb, zb, tile_rows(t)]
            ds = (weights[z, t].astype(jnp.float32) * (scratch[t] - delta)).astype(jnp.bfloat16)
            return mm(ds, q, ((1,), (0,))) * scaling, dq + mm(key_rows, ds, ((0,), (0,)))

        def own_tile(t, dq):
            dk, dq = find_terms(t, dq)
            own[KEY, z, tile_rows(t)] = dk
            return dq

        def far_tile(t, dq):
            dk, dq = find_terms(t, dq)
            pairs[KEY, t // 2 - 1, z, tile_rows(t)] = dk.astype(jnp.bfloat16)
            return dq

        dq = lax.fori_loop(0, 2, own_tile, jnp.zeros((HD, BLOCK), jnp.float32), unroll=2)
        dq = lax.fori_loop(2, 8, far_tile, dq, unroll=2)
        done[0, z] = (dq.T * scaling).astype(jnp.bfloat16)

        def send_rows(k, carry):
            send_out(0, z, lax.rem(h_me + k, nhead), q_out)
            return carry

        lax.fori_loop(0, nhead, send_rows, 0)

    level_loop(find_key_terms, 0, levels // 2 - 1)
    send_sums(VALUE)
    level_loop(find_key_terms, levels // 2 - 1, levels)
    send_terms(KEY)
    finish(VALUE, v_out)
    send_sums(KEY)
    finish(KEY, k_out)

    others_columns = pl.ds(0, (group - 1) * HD)
    await_bytes(lists.at[pl.ds(0, levels - 1)], list_send)
    for which, src in enumerate((k_in, v_in, q_in, g_in)):
        await_bytes(src.at[:, others_columns], in_send.at[which])
    for which in range(2):
        for side in range(2):
            await_bytes(keys.at[0], ring_send.at[which, side])
            await_bytes(keys.at[0, low], ring_send.at[which, 2 + side])
            for i in range(column_chunks):
                at = pl.ds(0, chunk)
                await_bytes(halves.at[which, side, :, at], part_send.at[which, side, i])
                await_bytes(parts.at[which, side, :, at], part_send.at[which, 2 + side, i])
    for which, out in enumerate((q_out, k_out, v_out)):
        await_bytes(out.at[:, others_columns], out_send.at[which])
        await_bytes(out, out_recv.at[which])


def per_device(queries, key_vectors, value_vectors, out_grad, chosen):
    levels = lax.axis_size("ctx") // RING
    nhead = lax.axis_size("head")
    bf = jnp.bfloat16
    f32 = jnp.float32
    dma = pltpu.SemaphoreType.DMA
    anywhere = pl.BlockSpec(memory_space=pl.ANY)
    slab = jax.ShapeDtypeStruct(queries.shape, bf)
    span = levels * PIECE
    scratch = [
        pltpu.VMEM((RING, levels, BLOCK, HD), bf),
        pltpu.VMEM((RING, levels, BLOCK, HD), bf),
        pltpu.VMEM((2, levels, BLOCK, HD), bf),
        pltpu.VMEM((levels, 8, BLOCK // 2, BLOCK), bf),
        pltpu.VMEM((8, BLOCK // 2, BLOCK), f32),
        pltpu.VMEM((2, TOPK, levels, BLOCK, HD), bf),
        pltpu.VMEM((2, levels, BLOCK, HD), f32),
        pltpu.VMEM((2, RING, levels, BLOCK, HD), bf),
        pltpu.VMEM((2, 2, levels // 2, BLOCK, HD), bf),
        pltpu.VMEM((2, 2, levels, BLOCK, HD), bf),
        pltpu.VMEM((3, levels, BLOCK, HD), bf),
        pltpu.VMEM((RING * span, TOPK * span), bf),
        pltpu.VMEM((8, 128), jnp.int32),
        pltpu.VMEM((levels, 8, 128), jnp.int32),
        pltpu.SMEM((levels, 8, 128), jnp.int32),
        dma,
        dma,
        dma,
        dma((4,)),
        dma((4, levels)),
        dma((2, 4)),
        dma((2, 4)),
        dma((2, 4, nhead // 2)),
        dma((2, 4, nhead // 2)),
        dma((3,)),
        dma((3,)),
    ]
    return pl.pallas_call(
        functools.partial(kernel, levels, nhead),
        out_shape=(slab, slab, slab),
        in_specs=[anywhere] * 4 + [pl.BlockSpec(memory_space=pltpu.SMEM)],
        out_specs=(anywhere,) * 3,
        scratch_shapes=scratch,
        compiler_params=pltpu.CompilerParams(
            collective_id=0, has_side_effects=True, vmem_limit_bytes=62 * 2**20
        ),
        name="sparse_attention_backward",
    )(queries, key_vectors, value_vectors, out_grad, chosen)


def solution(mesh):
    slabs = P(("ctx", "head"), None)
    return jax.shard_map(
        per_device,
        mesh=mesh,
        in_specs=(slabs, slabs, slabs, slabs, P("ctx", None)),
        out_specs=(slabs, slabs, slabs),
        check_vma=False,
    )
```

```python
import functools

import jax
import jax.numpy as jnp
from jax import lax
from jax.experimental import pallas as pl
from jax.experimental.pallas import tpu as pltpu
from jax.sharding import PartitionSpec as P

H = 64
HD = 128
BLOCK = 512
TOPK = 3
RING = 4
PIECE = 16
MESH = pl.DeviceIdType.MESH
LOG2E = 1.4426950408889634
masked_score = -1e30
KEY, VALUE = 0, 1
QUERY, GRAD = 0, 1


def mm(a, b, dims):
    return lax.dot_general(a, b, (dims, ((), ())), preferred_element_type=jnp.float32)


def kernel(
    levels,
    nhead,
    q_in,
    k_in,
    v_in,
    g_in,
    chosen_ref,
    q_out,
    k_out,
    v_out,
    keys,
    values,
    qg,
    weights,
    scratch,
    pairs,
    own,
    partial,
    halves,
    parts,
    done,
    choose,
    my_list,
    lists,
    targets,
    list_send,
    list_recv,
    list_local,
    in_send,
    in_recv,
    ring_send,
    ring_recv,
    part_send,
    part_recv,
    out_send,
    out_recv,
):
    c_me = lax.axis_index("ctx")
    h_me = lax.axis_index("head")
    z_me = c_me // RING
    x_me = lax.rem(c_me, RING)
    rows = BLOCK // nhead
    column_chunks = nhead
    chunk = BLOCK // column_chunks
    half = BLOCK // 2
    scaling = HD ** (-0.5)
    factor = scaling * LOG2E
    group = levels * nhead

    def remote(src, dst, send, recv, z_to, x_to, h_to):
        return pltpu.make_async_remote_copy(
            src_ref=src,
            dst_ref=dst,
            send_sem=send,
            recv_sem=recv,
            device_id=(z_to * RING + x_to, h_to),
            device_id_type=MESH,
        )

    def await_bytes(ref, sem):
        pltpu.make_async_copy(ref, ref, sem).wait()

    def near_level(k):
        step = jnp.where(lax.rem(k, 2) == 1, (k + 1) // 2, levels - k // 2)
        return lax.rem(z_me + step, levels)

    def group_peers(body):
        def step(k, carry):
            body(lax.rem(z_me + lax.rem(k, levels), levels), lax.rem(h_me + k // levels, nhead))
            return carry

        lax.fori_loop(1, group, step, 0)

    def near_peers_first(body):
        def step(k, carry):
            body(near_level(k // nhead), lax.rem(h_me + lax.rem(k, nhead), nhead))
            return carry

        lax.fori_loop(1, group, step, 0)

    def signal(z_to, x_to, h_to):
        pl.semaphore_signal(
            barrier, inc=1, device_id=(z_to * RING + x_to, h_to), device_id_type=MESH
        )

    barrier = pltpu.get_barrier_semaphore()
    group_peers(lambda z, h: signal(z, x_me, h))
    for x in (lax.rem(x_me + 1, RING), lax.rem(x_me + RING - 1, RING)):
        signal(z_me, x, h_me)
    pl.semaphore_wait(barrier, group + 1)

    def head_columns(z, h):
        return pl.ds(pl.multiple_of((z * nhead + h) * HD, HD), HD)

    def slab_rows(h):
        return pl.ds(pl.multiple_of(h * rows, rows), rows)

    def send_in(which, src, dst, peers):
        peers(
            lambda z, h: remote(
                src.at[:, head_columns(z, h)],
                dst.at[z_me, slab_rows(h_me)],
                in_send.at[which],
                in_recv.at[which, z_me],
                z,
                x_me,
                h,
            ).start()
        )
        pltpu.make_async_copy(
            src.at[:, head_columns(z_me, h_me)],
            dst.at[z_me, slab_rows(h_me)],
            in_recv.at[which, z_me],
        ).start()

    send_in(0, k_in, keys.at[x_me], group_peers)

    lane = lax.broadcasted_iota(jnp.int32, (8, 128), 1)
    my_list[...] = jnp.where(
        lane == 0, chosen_ref[0, 0], jnp.where(lane == 1, chosen_ref[0, 1], chosen_ref[0, 2])
    )

    def send_list(k, carry):
        remote(
            my_list, lists.at[z_me], list_send, list_recv, lax.rem(z_me + k, levels), x_me, h_me
        ).start()
        return carry

    lax.fori_loop(1, levels, send_list, 0)
    pltpu.make_async_copy(my_list, lists.at[z_me], list_recv).start()

    send_in(1, v_in, values.at[x_me], group_peers)
    send_in(2, q_in, qg.at[QUERY], near_peers_first)
    send_in(3, g_in, qg.at[GRAD], near_peers_first)

    await_bytes(lists, list_recv)
    to_scalars = pltpu.make_async_copy(lists, targets, list_local)
    to_scalars.start()
    to_scalars.wait()

    span = levels * PIECE
    for s in range(TOPK):
        lane = lax.broadcasted_iota(jnp.int32, (RING * span, span), 1)
        row = lax.broadcasted_iota(jnp.int32, (RING * span, span), 0)
        target = jnp.full((RING * span, span), -1, jnp.int32)
        for z in range(levels):
            target = jnp.where(lane // PIECE == z, targets[z, 0, s], target)
        block = lax.rem(row // PIECE, levels) * RING + row // span
        hit = (block == target) & (lax.rem(row, PIECE) == lax.rem(lane, PIECE))
        choose[:, s * span : (s + 1) * span] = jnp.where(hit, 1.0, 0.0).astype(jnp.bfloat16)

    right = lax.rem(x_me + 1, RING)
    left = lax.rem(x_me + RING - 1, RING)
    low = pl.ds(0, levels // 2)
    high = pl.ds(levels // 2, levels // 2)

    def ring_copy(src, dst, sems, to):
        return remote(src, dst, sems[0], sems[1], z_me, to, h_me)

    def share(which, blocks):
        def await_level(z, carry):
            await_bytes(blocks.at[x_me, z], in_recv.at[which, z])
            return carry

        lax.fori_loop(0, levels, await_level, 0)
        for side, to in enumerate((right, left)):
            ring_copy(
                blocks.at[x_me],
                blocks.at[x_me],
                (ring_send.at[which, side], ring_recv.at[which, side]),
                to,
            ).start()

    def pass_on(which, blocks):
        for side, (source, part, to) in enumerate(((left, low, right), (right, high, left))):
            await_bytes(blocks.at[source], ring_recv.at[which, side])
            ring_copy(
                blocks.at[source, part],
                blocks.at[source, part],
                (ring_send.at[which, 2 + side], ring_recv.at[which, 2 + side]),
                to,
            ).start()

    def await_shared(which, blocks):
        for side, part in enumerate((low, high)):
            await_bytes(blocks.at[0, part], ring_recv.at[which, 2 + side])

    def tile_rows(t):
        return pl.ds(pl.multiple_of(lax.rem(t, 2) * half, half), half)

    def tile_block(z, t):
        mine = z * RING + x_me
        block = jnp.where(t < 2, mine, targets[z, 0, jnp.maximum(t // 2 - 1, 0)])
        far = jnp.where(block != mine, -(2**20), 2**20)
        return lax.rem(block, RING), block // RING, jnp.where(t < 2, t * half, far)

    def folded(x, op):
        return op(x.reshape(half // 8, 8, BLOCK), axis=0)

    def level_loop(body, start=0, stop=levels):
        def step(k, carry):
            body(near_level(k))
            return carry

        lax.fori_loop(start, stop, step, 0)

    share(KEY, keys)
    pass_on(KEY, keys)
    share(VALUE, values)
    await_shared(KEY, keys)

    def find_weights(z):
        await_bytes(qg.at[QUERY, z], in_recv.at[2, z])
        q = qg[QUERY, z]

        def find_scores(t, largest):
            xb, zb, offset = tile_block(z, t)
            s = mm(keys[xb, zb, tile_rows(t)], q, ((1,), (1,)))
            key_at = lax.broadcasted_iota(jnp.int32, (half, BLOCK), 0) + offset
            query_at = lax.broadcasted_iota(jnp.int32, (half, BLOCK), 1)
            s = jnp.where(key_at <= query_at, s, masked_score)
            scratch[t] = s
            return jnp.maximum(largest, folded(s, jnp.max))

        largest = lax.fori_loop(
            0, 8, find_scores, jnp.full((8, BLOCK), masked_score, jnp.float32), unroll=8
        )
        largest = jnp.max(largest, axis=0, keepdims=True)

        def find_total(t, total):
            e = jnp.exp2((scratch[t] - largest) * factor)
            scratch[t] = e
            return total + folded(e, jnp.sum)

        total = lax.fori_loop(0, 8, find_total, jnp.zeros((8, BLOCK), jnp.float32), unroll=8)
        inverse = 1.0 / jnp.sum(total, axis=0, keepdims=True)

        def divide(t, carry):
            weights[z, t] = (scratch[t] * inverse).astype(jnp.bfloat16)
            return carry

        lax.fori_loop(0, 8, divide, 0, unroll=8)

    level_loop(find_weights, 0, levels // 2)
    pass_on(VALUE, values)
    level_loop(find_weights, levels // 2, levels)

    def find_value_terms(z):
        await_bytes(qg.at[GRAD, z], in_recv.at[3, z])
        g = qg[GRAD, z]

        def own_tile(t, carry):
            own[VALUE, z, tile_rows(t)] = mm(weights[z, t], g, ((1,), (0,)))
            return carry

        def far_tile(t, carry):
            term = mm(weights[z, t], g, ((1,), (0,)))
            pairs[VALUE, t // 2 - 1, z, tile_rows(t)] = term.astype(jnp.bfloat16)
            return carry

        lax.fori_loop(0, 2, own_tile, 0, unroll=2)
        lax.fori_loop(2, 8, far_tile, 0, unroll=6)

    level_loop(find_value_terms)

    across = lax.rem(x_me + 2, RING)

    def chunk_start(i):
        return lax.rem(h_me + i, column_chunks) * chunk

    def chunk_rows(i):
        return pl.ds(pl.multiple_of(chunk_start(i), chunk), chunk)

    def send_terms(which):
        for i in range(column_chunks):

            def add_rows(n, carry, i=i):
                first = chunk_start(i) + n * 2 * PIECE
                both = [
                    pl.ds(pl.multiple_of(first + m * PIECE, PIECE), PIECE) for m in range(2)
                ]
                terms = [pairs[which, :, :, at].reshape(TOPK * span, HD) for at in both]
                total = mm(choose[...], jnp.concatenate(terms, axis=1), ((1,), (0,)))
                total = total.astype(jnp.bfloat16)
                for m, at in enumerate(both):
                    partial[which, :, :, at] = total[:, m * HD : (m + 1) * HD].reshape(
                        RING, levels, PIECE, HD
                    )
                return carry

            lax.fori_loop(0, chunk // (2 * PIECE), add_rows, 0)
            at = chunk_rows(i)
            for side, (part, to) in enumerate(((low, right), (high, left))):
                ring_copy(
                    partial.at[which, across, part, at],
                    halves.at[which, side, :, at],
                    (part_send.at[which, side, i], part_recv.at[which, side, i]),
                    to,
                ).start()

    def send_sums(which):
        for i in range(column_chunks):
            at = chunk_rows(i)
            for side, (start, to) in enumerate(((0, right), (levels // 2, left))):
                await_bytes(halves.at[which, side, :, at], part_recv.at[which, side, i])

                def add_level(n, carry, at=at, side=side, start=start, to=to):
                    both = partial[which, to, start + n, at].astype(jnp.float32)
                    both = both + halves[which, side, n, at].astype(jnp.float32)
                    partial[which, to, start + n, at] = both.astype(jnp.bfloat16)
                    return carry

                lax.fori_loop(0, levels // 2, add_level, 0)
                ring_copy(
                    partial.at[which, to, :, at],
                    parts.at[which, side, :, at],
                    (part_send.at[which, 2 + side, i], part_recv.at[which, 2 + side, i]),
                    to,
                ).start()

    def send_out(which, z, h, dst):
        here = done.at[which, z, slab_rows(h)]
        there = dst.at[:, head_columns(z_me, h_me)]
        mine = (z == z_me) & (h == h_me)

        @pl.when(mine)
        def _():
            pltpu.make_async_copy(here, there, out_recv.at[which]).start()

        @pl.when(jnp.logical_not(mine))
        def _():
            remote(here, there, out_send.at[which], out_recv.at[which], z, x_me, h).start()

    def finish(which, dst):
        for i in range(column_chunks):
            at = chunk_rows(i)
            for side in range(2):
                await_bytes(parts.at[which, side, :, at], part_recv.at[which, 2 + side, i])

            def add_level(z, at=at):
                total = own[which, z, at] + partial[which, x_me, z, at].astype(jnp.float32)
                for side in range(2):
                    total = total + parts[which, side, z, at].astype(jnp.float32)
                done[1 + which, z, at] = total.astype(jnp.bfloat16)

            level_loop(add_level)

            def send_level(z, i=i):
                send_out(1 + which, z, lax.rem(h_me + i, nhead), dst)

            level_loop(send_level)

    send_terms(VALUE)

    await_shared(VALUE, values)

    def find_key_terms(z):
        q = qg[QUERY, z]
        g = qg[GRAD, z]

        def find_dprobs(t, delta):
            xb, zb, offset = tile_block(z, t)
            d = mm(values[xb, zb, tile_rows(t)], g, ((1,), (1,)))
            scratch[t] = d
            return delta + folded(weights[z, t].astype(jnp.float32) * d, jnp.sum)

        delta = lax.fori_loop(0, 8, find_dprobs, jnp.zeros((8, BLOCK), jnp.float32), unroll=8)
        delta = jnp.sum(delta, axis=0, keepdims=True)

        def find_terms(t, dq):
            xb, zb, offset = tile_block(z, t)
            key_rows = keys[xb, zb, tile_rows(t)]
            ds = (weights[z, t].astype(jnp.float32) * (scratch[t] - delta)).astype(jnp.bfloat16)
            return mm(ds, q, ((1,), (0,))) * scaling, dq + mm(key_rows, ds, ((0,), (0,)))

        def own_tile(t, dq):
            dk, dq = find_terms(t, dq)
            own[KEY, z, tile_rows(t)] = dk
            return dq

        def far_tile(t, dq):
            dk, dq = find_terms(t, dq)
            pairs[KEY, t // 2 - 1, z, tile_rows(t)] = dk.astype(jnp.bfloat16)
            return dq

        dq = lax.fori_loop(0, 2, own_tile, jnp.zeros((HD, BLOCK), jnp.float32), unroll=2)
        dq = lax.fori_loop(2, 8, far_tile, dq, unroll=6)
        done[0, z] = (dq.T * scaling).astype(jnp.bfloat16)

        def send_rows(k, carry):
            send_out(0, z, lax.rem(h_me + k, nhead), q_out)
            return carry

        lax.fori_loop(0, nhead, send_rows, 0)

    level_loop(find_key_terms, 0, levels // 2 - 1)
    send_sums(VALUE)
    level_loop(find_key_terms, levels // 2 - 1, levels)
    send_terms(KEY)
    finish(VALUE, v_out)
    send_sums(KEY)
    finish(KEY, k_out)

    others_columns = pl.ds(0, (group - 1) * HD)
    await_bytes(lists.at[pl.ds(0, levels - 1)], list_send)
    for which, src in enumerate((k_in, v_in, q_in, g_in)):
        await_bytes(src.at[:, others_columns], in_send.at[which])
    for which in range(2):
        for side in range(2):
            await_bytes(keys.at[0], ring_send.at[which, side])
            await_bytes(keys.at[0, low], ring_send.at[which, 2 + side])
            for i in range(column_chunks):
                at = pl.ds(0, chunk)
                await_bytes(halves.at[which, side, :, at], part_send.at[which, side, i])
                await_bytes(parts.at[which, side, :, at], part_send.at[which, 2 + side, i])
    for which, out in enumerate((q_out, k_out, v_out)):
        await_bytes(out.at[:, others_columns], out_send.at[which])
        await_bytes(out, out_recv.at[which])


def per_device(queries, key_vectors, value_vectors, out_grad, chosen):
    levels = lax.axis_size("ctx") // RING
    nhead = lax.axis_size("head")
    bf = jnp.bfloat16
    f32 = jnp.float32
    dma = pltpu.SemaphoreType.DMA
    anywhere = pl.BlockSpec(memory_space=pl.ANY)
    slab = jax.ShapeDtypeStruct(queries.shape, bf)
    span = levels * PIECE
    scratch = [
        pltpu.VMEM((RING, levels, BLOCK, HD), bf),
        pltpu.VMEM((RING, levels, BLOCK, HD), bf),
        pltpu.VMEM((2, levels, BLOCK, HD), bf),
        pltpu.VMEM((levels, 8, BLOCK // 2, BLOCK), bf),
        pltpu.VMEM((8, BLOCK // 2, BLOCK), f32),
        pltpu.VMEM((2, TOPK, levels, BLOCK, HD), bf),
        pltpu.VMEM((2, levels, BLOCK, HD), f32),
        pltpu.VMEM((2, RING, levels, BLOCK, HD), bf),
        pltpu.VMEM((2, 2, levels // 2, BLOCK, HD), bf),
        pltpu.VMEM((2, 2, levels, BLOCK, HD), bf),
        pltpu.VMEM((3, levels, BLOCK, HD), bf),
        pltpu.VMEM((RING * span, TOPK * span), bf),
        pltpu.VMEM((8, 128), jnp.int32),
        pltpu.VMEM((levels, 8, 128), jnp.int32),
        pltpu.SMEM((levels, 8, 128), jnp.int32),
        dma,
        dma,
        dma,
        dma((4,)),
        dma((4, levels)),
        dma((2, 4)),
        dma((2, 4)),
        dma((2, 4, nhead)),
        dma((2, 4, nhead)),
        dma((3,)),
        dma((3,)),
    ]
    return pl.pallas_call(
        functools.partial(kernel, levels, nhead),
        out_shape=(slab, slab, slab),
        in_specs=[anywhere] * 4 + [pl.BlockSpec(memory_space=pltpu.SMEM)],
        out_specs=(anywhere,) * 3,
        scratch_shapes=scratch,
        compiler_params=pltpu.CompilerParams(
            collective_id=0, has_side_effects=True, vmem_limit_bytes=62 * 2**20
        ),
        name="sparse_attention_backward",
    )(queries, key_vectors, value_vectors, out_grad, chosen)


def solution(mesh):
    slabs = P(("ctx", "head"), None)
    return jax.shard_map(
        per_device,
        mesh=mesh,
        in_specs=(slabs, slabs, slabs, slabs, P("ctx", None)),
        out_specs=(slabs, slabs, slabs),
        check_vma=False,
    )
```

```python
import functools

import jax
import jax.numpy as jnp
from jax import lax
from jax.experimental import pallas as pl
from jax.experimental.pallas import tpu as pltpu
from jax.sharding import PartitionSpec as P

H = 64
HD = 128
BLOCK = 512
TOPK = 3
RING = 4
PIECE = 16
MESH = pl.DeviceIdType.MESH
LOG2E = 1.4426950408889634
masked_score = -1e30
KEY, VALUE = 0, 1
QUERY, GRAD = 0, 1


def mm(a, b, dims):
    return lax.dot_general(a, b, (dims, ((), ())), preferred_element_type=jnp.float32)


def kernel(
    levels,
    nhead,
    q_in,
    k_in,
    v_in,
    g_in,
    chosen_ref,
    q_out,
    k_out,
    v_out,
    keys,
    values,
    qg,
    weights,
    scratch,
    pairs,
    own,
    partial,
    halves,
    parts,
    done,
    choose,
    my_list,
    lists,
    targets,
    list_send,
    list_recv,
    list_local,
    in_send,
    in_recv,
    ring_send,
    ring_recv,
    part_send,
    part_recv,
    out_send,
    out_recv,
):
    c_me = lax.axis_index("ctx")
    h_me = lax.axis_index("head")
    z_me = c_me // RING
    x_me = lax.rem(c_me, RING)
    rows = BLOCK // nhead
    column_chunks = nhead
    chunk = BLOCK // column_chunks
    half = BLOCK // 2
    scaling = HD ** (-0.5)
    factor = scaling * LOG2E
    group = levels * nhead

    def remote(src, dst, send, recv, z_to, x_to, h_to):
        return pltpu.make_async_remote_copy(
            src_ref=src,
            dst_ref=dst,
            send_sem=send,
            recv_sem=recv,
            device_id=(z_to * RING + x_to, h_to),
            device_id_type=MESH,
        )

    def await_bytes(ref, sem):
        pltpu.make_async_copy(ref, ref, sem).wait()

    def near_level(k):
        step = jnp.where(lax.rem(k, 2) == 1, (k + 1) // 2, levels - k // 2)
        return lax.rem(z_me + step, levels)

    def group_peers(body):
        def step(k, carry):
            body(lax.rem(z_me + lax.rem(k, levels), levels), lax.rem(h_me + k // levels, nhead))
            return carry

        lax.fori_loop(1, group, step, 0)

    def near_peers_first(body):
        def step(k, carry):
            body(near_level(k // nhead), lax.rem(h_me + lax.rem(k, nhead), nhead))
            return carry

        lax.fori_loop(1, group, step, 0)

    def signal(z_to, x_to, h_to):
        pl.semaphore_signal(
            barrier, inc=1, device_id=(z_to * RING + x_to, h_to), device_id_type=MESH
        )

    barrier = pltpu.get_barrier_semaphore()
    group_peers(lambda z, h: signal(z, x_me, h))
    for x in (lax.rem(x_me + 1, RING), lax.rem(x_me + RING - 1, RING)):
        signal(z_me, x, h_me)
    pl.semaphore_wait(barrier, group + 1)

    def head_columns(z, h):
        return pl.ds(pl.multiple_of((z * nhead + h) * HD, HD), HD)

    def slab_rows(h):
        return pl.ds(pl.multiple_of(h * rows, rows), rows)

    def send_in(which, src, dst, peers):
        peers(
            lambda z, h: remote(
                src.at[:, head_columns(z, h)],
                dst.at[z_me, slab_rows(h_me)],
                in_send.at[which],
                in_recv.at[which, z_me],
                z,
                x_me,
                h,
            ).start()
        )
        pltpu.make_async_copy(
            src.at[:, head_columns(z_me, h_me)],
            dst.at[z_me, slab_rows(h_me)],
            in_recv.at[which, z_me],
        ).start()

    send_in(0, k_in, keys.at[x_me], group_peers)

    lane = lax.broadcasted_iota(jnp.int32, (8, 128), 1)
    my_list[...] = jnp.where(
        lane == 0, chosen_ref[0, 0], jnp.where(lane == 1, chosen_ref[0, 1], chosen_ref[0, 2])
    )

    def send_list(k, carry):
        remote(
            my_list, lists.at[z_me], list_send, list_recv, lax.rem(z_me + k, levels), x_me, h_me
        ).start()
        return carry

    lax.fori_loop(1, levels, send_list, 0)
    pltpu.make_async_copy(my_list, lists.at[z_me], list_recv).start()

    send_in(1, v_in, values.at[x_me], group_peers)
    send_in(2, q_in, qg.at[QUERY], near_peers_first)
    send_in(3, g_in, qg.at[GRAD], near_peers_first)

    await_bytes(lists, list_recv)
    to_scalars = pltpu.make_async_copy(lists, targets, list_local)
    to_scalars.start()
    to_scalars.wait()

    span = levels * PIECE
    for s in range(TOPK):
        lane = lax.broadcasted_iota(jnp.int32, (RING * span, span), 1)
        row = lax.broadcasted_iota(jnp.int32, (RING * span, span), 0)
        target = jnp.full((RING * span, span), -1, jnp.int32)
        for z in range(levels):
            target = jnp.where(lane // PIECE == z, targets[z, 0, s], target)
        block = lax.rem(row // PIECE, levels) * RING + row // span
        hit = (block == target) & (lax.rem(row, PIECE) == lax.rem(lane, PIECE))
        choose[:, s * span : (s + 1) * span] = jnp.where(hit, 1.0, 0.0).astype(jnp.bfloat16)

    right = lax.rem(x_me + 1, RING)
    left = lax.rem(x_me + RING - 1, RING)
    low = pl.ds(0, levels // 2)
    high = pl.ds(levels // 2, levels // 2)

    def ring_copy(src, dst, sems, to):
        return remote(src, dst, sems[0], sems[1], z_me, to, h_me)

    def share(which, blocks):
        def await_level(z, carry):
            await_bytes(blocks.at[x_me, z], in_recv.at[which, z])
            return carry

        lax.fori_loop(0, levels, await_level, 0)
        for side, to in enumerate((right, left)):
            ring_copy(
                blocks.at[x_me],
                blocks.at[x_me],
                (ring_send.at[which, side], ring_recv.at[which, side]),
                to,
            ).start()

    def pass_on(which, blocks):
        for side, (source, part, to) in enumerate(((left, low, right), (right, high, left))):
            await_bytes(blocks.at[source], ring_recv.at[which, side])
            ring_copy(
                blocks.at[source, part],
                blocks.at[source, part],
                (ring_send.at[which, 2 + side], ring_recv.at[which, 2 + side]),
                to,
            ).start()

    def await_shared(which, blocks):
        for side, part in enumerate((low, high)):
            await_bytes(blocks.at[0, part], ring_recv.at[which, 2 + side])

    def tile_rows(t):
        return pl.ds(pl.multiple_of(lax.rem(t, 2) * half, half), half)

    def tile_block(z, t):
        mine = z * RING + x_me
        block = jnp.where(t < 2, mine, targets[z, 0, jnp.maximum(t // 2 - 1, 0)])
        far = jnp.where(block != mine, -(2**20), 2**20)
        return lax.rem(block, RING), block // RING, jnp.where(t < 2, t * half, far)

    def folded(x, op):
        return op(x.reshape(half // 8, 8, BLOCK), axis=0)

    def level_loop(body, start=0, stop=levels):
        def step(k, carry):
            body(near_level(k))
            return carry

        lax.fori_loop(start, stop, step, 0)

    def far_levels_first(body):
        def step(k, carry):
            body(near_level(levels - 1 - k))
            return carry

        lax.fori_loop(0, levels, step, 0)

    share(KEY, keys)
    pass_on(KEY, keys)
    share(VALUE, values)
    await_shared(KEY, keys)

    def find_weights(z):
        await_bytes(qg.at[QUERY, z], in_recv.at[2, z])
        q = qg[QUERY, z]

        def find_scores(t, largest):
            xb, zb, offset = tile_block(z, t)
            s = mm(keys[xb, zb, tile_rows(t)], q, ((1,), (1,)))
            key_at = lax.broadcasted_iota(jnp.int32, (half, BLOCK), 0) + offset
            query_at = lax.broadcasted_iota(jnp.int32, (half, BLOCK), 1)
            s = jnp.where(key_at <= query_at, s, masked_score)
            scratch[t] = s
            return jnp.maximum(largest, folded(s, jnp.max))

        largest = lax.fori_loop(
            0, 8, find_scores, jnp.full((8, BLOCK), masked_score, jnp.float32), unroll=8
        )
        largest = jnp.max(largest, axis=0, keepdims=True)

        def find_total(t, total):
            e = jnp.exp2((scratch[t] - largest) * factor)
            scratch[t] = e
            return total + folded(e, jnp.sum)

        total = lax.fori_loop(0, 8, find_total, jnp.zeros((8, BLOCK), jnp.float32), unroll=8)
        inverse = 1.0 / jnp.sum(total, axis=0, keepdims=True)

        def divide(t, carry):
            weights[z, t] = (scratch[t] * inverse).astype(jnp.bfloat16)
            return carry

        lax.fori_loop(0, 8, divide, 0, unroll=8)

    level_loop(find_weights, 0, levels // 2)
    pass_on(VALUE, values)
    level_loop(find_weights, levels // 2, levels)

    def find_value_terms(z):
        await_bytes(qg.at[GRAD, z], in_recv.at[3, z])
        g = qg[GRAD, z]

        def own_tile(t, carry):
            own[VALUE, z, tile_rows(t)] = mm(weights[z, t], g, ((1,), (0,)))
            return carry

        def far_tile(t, carry):
            term = mm(weights[z, t], g, ((1,), (0,)))
            pairs[VALUE, t // 2 - 1, z, tile_rows(t)] = term.astype(jnp.bfloat16)
            return carry

        lax.fori_loop(0, 2, own_tile, 0, unroll=2)
        lax.fori_loop(2, 8, far_tile, 0, unroll=6)

    level_loop(find_value_terms)

    across = lax.rem(x_me + 2, RING)

    def chunk_start(i):
        return lax.rem(h_me + i, column_chunks) * chunk

    def chunk_rows(i):
        return pl.ds(pl.multiple_of(chunk_start(i), chunk), chunk)

    def send_terms(which):
        for i in range(column_chunks):

            def add_rows(n, carry, i=i):
                first = chunk_start(i) + n * 2 * PIECE
                both = [
                    pl.ds(pl.multiple_of(first + m * PIECE, PIECE), PIECE) for m in range(2)
                ]
                terms = [pairs[which, :, :, at].reshape(TOPK * span, HD) for at in both]
                total = mm(choose[...], jnp.concatenate(terms, axis=1), ((1,), (0,)))
                total = total.astype(jnp.bfloat16)
                for m, at in enumerate(both):
                    partial[which, :, :, at] = total[:, m * HD : (m + 1) * HD].reshape(
                        RING, levels, PIECE, HD
                    )
                return carry

            lax.fori_loop(0, chunk // (2 * PIECE), add_rows, 0)
            at = chunk_rows(i)
            for side, (part, to) in enumerate(((low, right), (high, left))):
                ring_copy(
                    partial.at[which, across, part, at],
                    halves.at[which, side, :, at],
                    (part_send.at[which, side, i], part_recv.at[which, side, i]),
                    to,
                ).start()

    def send_sums(which, i):
        at = chunk_rows(i)
        for side, (start, to) in enumerate(((0, right), (levels // 2, left))):
            await_bytes(halves.at[which, side, :, at], part_recv.at[which, side, i])

            def add_level(n, carry, at=at, side=side, start=start, to=to):
                both = partial[which, to, start + n, at].astype(jnp.float32)
                both = both + halves[which, side, n, at].astype(jnp.float32)
                partial[which, to, start + n, at] = both.astype(jnp.bfloat16)
                return carry

            lax.fori_loop(0, levels // 2, add_level, 0)
            ring_copy(
                partial.at[which, to, :, at],
                parts.at[which, side, :, at],
                (part_send.at[which, 2 + side, i], part_recv.at[which, 2 + side, i]),
                to,
            ).start()

    def send_out(which, z, h, dst):
        here = done.at[which, z, slab_rows(h)]
        there = dst.at[:, head_columns(z_me, h_me)]
        mine = (z == z_me) & (h == h_me)

        @pl.when(mine)
        def _():
            pltpu.make_async_copy(here, there, out_recv.at[which]).start()

        @pl.when(jnp.logical_not(mine))
        def _():
            remote(here, there, out_send.at[which], out_recv.at[which], z, x_me, h).start()

    def finish(which, dst, i):
        at = chunk_rows(i)
        for side in range(2):
            await_bytes(parts.at[which, side, :, at], part_recv.at[which, 2 + side, i])

        def add_level(z, at=at):
            total = own[which, z, at] + partial[which, x_me, z, at].astype(jnp.float32)
            for side in range(2):
                total = total + parts[which, side, z, at].astype(jnp.float32)
            done[1 + which, z, at] = total.astype(jnp.bfloat16)

        level_loop(add_level)

        def send_level(z, i=i):
            send_out(1 + which, z, lax.rem(h_me + i, nhead), dst)

        far_levels_first(send_level)

    send_terms(VALUE)

    await_shared(VALUE, values)

    def find_key_terms(z):
        q = qg[QUERY, z]
        g = qg[GRAD, z]

        def find_dprobs(t, delta):
            xb, zb, offset = tile_block(z, t)
            d = mm(values[xb, zb, tile_rows(t)], g, ((1,), (1,)))
            scratch[t] = d
            return delta + folded(weights[z, t].astype(jnp.float32) * d, jnp.sum)

        delta = lax.fori_loop(0, 8, find_dprobs, jnp.zeros((8, BLOCK), jnp.float32), unroll=8)
        delta = jnp.sum(delta, axis=0, keepdims=True)

        def find_terms(t, dq):
            xb, zb, offset = tile_block(z, t)
            key_rows = keys[xb, zb, tile_rows(t)]
            ds = (weights[z, t].astype(jnp.float32) * (scratch[t] - delta)).astype(jnp.bfloat16)
            return mm(ds, q, ((1,), (0,))) * scaling, dq + mm(key_rows, ds, ((0,), (0,)))

        def own_tile(t, dq):
            dk, dq = find_terms(t, dq)
            own[KEY, z, tile_rows(t)] = dk
            return dq

        def far_tile(t, dq):
            dk, dq = find_terms(t, dq)
            pairs[KEY, t // 2 - 1, z, tile_rows(t)] = dk.astype(jnp.bfloat16)
            return dq

        dq = lax.fori_loop(0, 2, own_tile, jnp.zeros((HD, BLOCK), jnp.float32), unroll=2)
        dq = lax.fori_loop(2, 8, far_tile, dq, unroll=6)
        done[0, z] = (dq.T * scaling).astype(jnp.bfloat16)

        def send_rows(k, carry):
            send_out(0, z, lax.rem(h_me + k, nhead), q_out)
            return carry

        lax.fori_loop(0, nhead, send_rows, 0)

    def key_level(k, carry):
        find_key_terms(near_level(k))

        @pl.when(k == levels // 2 - 1)
        def _():
            for i in range(column_chunks):
                send_sums(VALUE, i)

        return carry

    lax.fori_loop(0, levels, key_level, 0)
    send_terms(KEY)
    for i in range(column_chunks):
        finish(VALUE, v_out, i)
        send_sums(KEY, i)
    for i in range(column_chunks):
        finish(KEY, k_out, i)

    others_columns = pl.ds(0, (group - 1) * HD)
    await_bytes(lists.at[pl.ds(0, levels - 1)], list_send)
    for which, src in enumerate((k_in, v_in, q_in, g_in)):
        await_bytes(src.at[:, others_columns], in_send.at[which])
    for which in range(2):
        for side in range(2):
            await_bytes(keys.at[0], ring_send.at[which, side])
            await_bytes(keys.at[0, low], ring_send.at[which, 2 + side])
            for i in range(column_chunks):
                at = pl.ds(0, chunk)
                await_bytes(halves.at[which, side, :, at], part_send.at[which, side, i])
                await_bytes(parts.at[which, side, :, at], part_send.at[which, 2 + side, i])
    for which, out in enumerate((q_out, k_out, v_out)):
        await_bytes(out.at[:, others_columns], out_send.at[which])
        await_bytes(out, out_recv.at[which])


def per_device(queries, key_vectors, value_vectors, out_grad, chosen):
    levels = lax.axis_size("ctx") // RING
    nhead = lax.axis_size("head")
    bf = jnp.bfloat16
    f32 = jnp.float32
    dma = pltpu.SemaphoreType.DMA
    anywhere = pl.BlockSpec(memory_space=pl.ANY)
    slab = jax.ShapeDtypeStruct(queries.shape, bf)
    span = levels * PIECE
    scratch = [
        pltpu.VMEM((RING, levels, BLOCK, HD), bf),
        pltpu.VMEM((RING, levels, BLOCK, HD), bf),
        pltpu.VMEM((2, levels, BLOCK, HD), bf),
        pltpu.VMEM((levels, 8, BLOCK // 2, BLOCK), bf),
        pltpu.VMEM((8, BLOCK // 2, BLOCK), f32),
        pltpu.VMEM((2, TOPK, levels, BLOCK, HD), bf),
        pltpu.VMEM((2, levels, BLOCK, HD), f32),
        pltpu.VMEM((2, RING, levels, BLOCK, HD), bf),
        pltpu.VMEM((2, 2, levels // 2, BLOCK, HD), bf),
        pltpu.VMEM((2, 2, levels, BLOCK, HD), bf),
        pltpu.VMEM((3, levels, BLOCK, HD), bf),
        pltpu.VMEM((RING * span, TOPK * span), bf),
        pltpu.VMEM((8, 128), jnp.int32),
        pltpu.VMEM((levels, 8, 128), jnp.int32),
        pltpu.SMEM((levels, 8, 128), jnp.int32),
        dma,
        dma,
        dma,
        dma((4,)),
        dma((4, levels)),
        dma((2, 4)),
        dma((2, 4)),
        dma((2, 4, nhead)),
        dma((2, 4, nhead)),
        dma((3,)),
        dma((3,)),
    ]
    return pl.pallas_call(
        functools.partial(kernel, levels, nhead),
        out_shape=(slab, slab, slab),
        in_specs=[anywhere] * 4 + [pl.BlockSpec(memory_space=pltpu.SMEM)],
        out_specs=(anywhere,) * 3,
        scratch_shapes=scratch,
        compiler_params=pltpu.CompilerParams(
            collective_id=0, has_side_effects=True, vmem_limit_bytes=62 * 2**20
        ),
        name="sparse_attention_backward",
    )(queries, key_vectors, value_vectors, out_grad, chosen)


def solution(mesh):
    slabs = P(("ctx", "head"), None)
    return jax.shard_map(
        per_device,
        mesh=mesh,
        in_specs=(slabs, slabs, slabs, slabs, P("ctx", None)),
        out_specs=(slabs, slabs, slabs),
        check_vma=False,
    )
```
